32 devices in a mesh: expert: 4 (over x, core), dp: 8 (over z, y).
Axes of the slice: x: 2, y: 2, z: 4, core: 2. Of those that a mesh axis runs over, the one named last changes fastest.
Arguments:
- tokens: bfloat16 [4096, 1280], P(('expert', 'dp')), may hold values from -6 to 6
- expert_ids: int32 [4096], P(('expert', 'dp')), may hold values from 0 to 15, as said below
- up_weight: bfloat16 [16, 1280, 4096], P('expert', None, 'dp'), may hold values from -0.15625 to 0.15625
- down_weight: bfloat16 [16, 4096, 1280], P('expert', 'dp'), may hold values from -0.09375 to 0.09375
- out_grad: bfloat16 [4096, 1280], P(('expert', 'dp')), may hold values from -0.1875 to 0.1875
Outputs:
- expert_out: bfloat16 [4096, 1280], P(('expert', 'dp'))
- up_grad: bfloat16 [16, 1280, 4096], P('expert', None, 'dp')
- down_grad: bfloat16 [16, 4096, 1280], P('expert', 'dp')
The draws below stay inside these ranges and needn't reach their ends.
Inputs may be any that keep to these rules, and one draw needn't show every extreme that they name: `expert_ids`: within each aligned block of 128 tokens (the tokens of one device) no expert id appears more than 10 times, and in every draw one expert appears exactly 10 times in every block.
All inputs are finite; a program needn't handle non-finite values.
Results may differ from the reference program's by a relative error of at most 0.005.
Values may be sent and summed in bfloat16 or wider, within the bound.
No kernel may reach another device: no remote copies, remote signals or barrier semaphores. Data moves between devices by JAX's collectives and lax.ppermute only.
A program may use at most 128 MiB of HBM per device.

```python
import math
import jax
import jax.numpy as jnp
from jax import lax

D = 1280
FF = 4096
TOK_DEV = 128
EXPERTS = 16
CAP = 10
TOKENS = 4096
N_DP = 8


def draw_expert_ids(key, part):
    blocks = TOKENS // TOK_DEV
    hottest = jax.random.randint(jax.random.fold_in(key, 1), (), 0, EXPERTS)
    levels = jax.random.randint(jax.random.fold_in(key, 2), (EXPERTS,), 0, 4)
    slot_count = EXPERTS * CAP
    order_index = jnp.arange(slot_count, dtype=jnp.int32).reshape(EXPERTS, CAP)
    expert_index = jnp.arange(EXPERTS, dtype=jnp.int32)[:, None]

    def one_block(block_key):
        first_key, second_key = jax.random.split(block_key)
        noise = jax.random.randint(first_key, (EXPERTS, CAP), 0, 2 ** 16)
        scores = (noise + levels[:, None] * 2 ** 14) * slot_count + order_index
        scores = jnp.where(expert_index == hottest, 2 ** 30 + order_index, scores)
        unused, chosen = lax.top_k(scores.reshape(-1), TOK_DEV)
        owners = (chosen // CAP).astype(jnp.int32)
        return jax.random.permutation(second_key, owners)
    block_keys = jax.vmap(lambda index: jax.random.fold_in(key, index + 10))(jnp.arange(blocks))
    return jax.vmap(one_block)(block_keys).reshape(-1).astype(jnp.int32)


def steps_of(stream_key, extent, pieces, least, top_value):
    factor_of = 1.0
    for axis_at, shards_of in pieces:
        draws = jax.random.uniform(jax.random.fold_in(jax.random.fold_in(stream_key, 6), axis_at), (shards_of,), jnp.float32, least / len(pieces), top_value / len(pieces))
        factor_of = factor_of * jnp.repeat(jnp.exp(draws), extent[axis_at] // shards_of).reshape((-1,) + (1,) * (len(extent) - 1 - axis_at))
    return factor_of


def bell_draw(stream_key, shape, width, most, shards=(), kind=jnp.bfloat16):
    entries = width * jax.random.normal(stream_key, shape, jnp.float32)
    if shards:
        entries = entries * steps_of(stream_key, shape, shards, -0.22, 0.18)
    return jnp.clip(entries, -most, most).astype(kind)


def setup_inputs(seed: int = 0) -> dict:
    streams_of = jax.random.split(jax.random.key(seed), 6)
    tokens = bell_draw(streams_of[0], (TOKENS, D), 1.0, 6.0, ((0, 32),))
    expert_ids = draw_expert_ids(jax.random.fold_in(streams_of[5], 71), 0)
    up_weight = bell_draw(streams_of[2], (EXPERTS, D, FF), D ** -0.5, 0.15625, ((0, 4), (2, 8)))
    down_weight = bell_draw(streams_of[3], (EXPERTS, FF, D), FF ** -0.5, 0.09375, ((0, 4), (1, 8)))
    out_grad = bell_draw(streams_of[4], (TOKENS, D), ((TOK_DEV * N_DP) ** -0.5), 0.1875, ((0, 32),))
    return {"tokens": tokens, "expert_ids": expert_ids, "up_weight": up_weight, "down_weight": down_weight, "out_grad": out_grad}


gelu_scale = math.sqrt(2.0 / math.pi)
cubic_term = 0.044715

def gelu_value(values):
    inner_arg = gelu_scale * (values + cubic_term * values * values * values)
    return 0.5 * values * (1.0 + jnp.tanh(inner_arg))

def gelu_slope(values):
    tangent = jnp.tanh(gelu_scale * (values + cubic_term * values * values * values))
    return 0.5 * (1.0 + tangent) + 0.5 * values * (1.0 - tangent * tangent) * gelu_scale * (1.0 + 3.0 * cubic_term * values * values)

def per_expert(inputs):
    rows_tok, rows_grad, w_in, w_out = inputs
    hidden_pre = jnp.dot(rows_tok, w_in, preferred_element_type=jnp.float32)
    active = gelu_value(hidden_pre).astype(jnp.bfloat16)
    result = jnp.dot(active, w_out, preferred_element_type=jnp.float32).astype(jnp.bfloat16)
    back_grad = jnp.dot(rows_grad, w_out.T, preferred_element_type=jnp.float32)
    pre_grad = (back_grad * gelu_slope(hidden_pre)).astype(jnp.bfloat16)
    down_part = jnp.dot(active.T, rows_grad, preferred_element_type=jnp.float32).astype(jnp.bfloat16)
    up_part = jnp.dot(rows_tok.T, pre_grad, preferred_element_type=jnp.float32).astype(jnp.bfloat16)
    return (result, up_part, down_part)

def reference(tokens, expert_ids, up_weight, down_weight, out_grad):
    blocks = TOKENS // TOK_DEV
    block_ids = expert_ids.reshape(blocks, TOK_DEV)
    onehot = (block_ids[:, :, None] == jnp.arange(EXPERTS, dtype=jnp.int32)[None, None, :]).astype(jnp.int32)
    ranks = jnp.cumsum(onehot, axis=1) - 1
    slot_index = lax.optimization_barrier(jnp.sum(onehot * ranks, axis=2))
    block_index = jnp.arange(blocks, dtype=jnp.int32)[:, None]
    flat_target = ((block_ids * blocks + block_index) * CAP + slot_index).reshape(-1).astype(jnp.int32)
    total_rows = EXPERTS * blocks * CAP
    tok_buffer = jnp.zeros((total_rows, D), jnp.bfloat16).at[flat_target].set(tokens)
    grad_buffer = jnp.zeros((total_rows, D), jnp.bfloat16).at[flat_target].set(out_grad)
    tok_buffer = tok_buffer.reshape(EXPERTS, blocks * CAP, D)
    grad_buffer = grad_buffer.reshape(EXPERTS, blocks * CAP, D)
    results, up_grad, down_grad = lax.map(per_expert, (tok_buffer, grad_buffer, up_weight, down_weight))
    expert_out = results.reshape(total_rows, D)[flat_target]
    return (expert_out, up_grad, down_grad)
```

```python
import math

import jax
import jax.numpy as jnp
from jax import lax
from jax.sharding import PartitionSpec as P

gelu_scale = math.sqrt(2.0 / math.pi)
cubic_term = 0.044715


def gelu_value(values):
    inner_arg = gelu_scale * (values + cubic_term * values * values * values)
    return 0.5 * values * (1.0 + jnp.tanh(inner_arg))


def gelu_slope(values):
    tangent = jnp.tanh(gelu_scale * (values + cubic_term * values * values * values))
    return 0.5 * (1.0 + tangent) + 0.5 * values * (1.0 - tangent * tangent) * gelu_scale * (
        1.0 + 3.0 * cubic_term * values * values
    )


def grid_of(n):
    cols = 1
    while cols * cols * 4 <= n and n % (cols * 2) == 0:
        cols *= 2
    return n // cols, cols


def ring_z(value, step):
    n = lax.axis_size("dp")
    rows, cols = grid_of(n)
    perm = [(i, ((i // cols + step) % rows) * cols + i % cols) for i in range(n)]
    return lax.ppermute(value, "dp", perm)


def ring_y(value, step):
    n = lax.axis_size("dp")
    cols = grid_of(n)[1]
    perm = [(i, i // cols * cols + (i % cols + step) % cols) for i in range(n)]
    return lax.ppermute(value, "dp", perm)


def swap_expert(value, mask):
    n = lax.axis_size("expert")
    return lax.ppermute(value, "expert", [(i, i ^ mask) for i in range(n)])


def exchange(packed):
    return [packed[0]] + [swap_expert(packed[m], m) for m in range(1, packed.shape[0])]


def gather_dp(block):
    rows, cols = grid_of(lax.axis_size("dp"))
    blocks = []
    for k in range(rows):
        line = [block]
        for _ in range(cols - 1):
            line.append(ring_y(line[-1], 1))
        blocks.append(line)
        if k < rows - 1:
            block = ring_z(block, 1)
    return blocks


def scatter_dp(parts):
    rows, cols = grid_of(lax.axis_size("dp"))
    total = None
    for k in reversed(range(rows)):
        line = parts[k][cols - 1]
        for j in reversed(range(cols - 1)):
            line = ring_y(line.astype(jnp.bfloat16), -1).astype(jnp.float32) + parts[k][j]
        if total is None:
            total = line
        else:
            total = ring_z(total.astype(jnp.bfloat16), -1).astype(jnp.float32) + line
    return total


def on_device(tokens, expert_ids, up_weight, down_weight, out_grad):
    owners = lax.axis_size("expert")
    rows, cols = grid_of(lax.axis_size("dp"))
    local_experts = up_weight.shape[0]
    all_experts = owners * local_experts
    tok_rows, width = tokens.shape
    capacity = 5 * tok_rows // (4 * all_experts)
    slots = all_experts * capacity
    me = lax.axis_index("expert")
    index = jnp.arange(tok_rows, dtype=jnp.int32)
    earlier = (expert_ids[:, None] == expert_ids[None, :]) & (index[:, None] < index[None, :])
    slot_index = jnp.sum(earlier.astype(jnp.int32), axis=0)
    owner_id = expert_ids // local_experts
    local_id = expert_ids % local_experts
    target = ((owner_id ^ me) * local_experts + local_id) * capacity + slot_index
    place = (target[None, :] == jnp.arange(slots, dtype=jnp.int32)[:, None]).astype(jnp.bfloat16)

    def dispatch(values):
        packed = jnp.dot(place, values, preferred_element_type=jnp.float32).astype(values.dtype)
        got = exchange(packed.reshape(owners, local_experts, capacity, width))
        return jnp.stack(got, axis=1).reshape(local_experts, owners * capacity, width)

    def rows_of(blocks):
        return jnp.concatenate([b for line in blocks for b in line], axis=1)

    rows_tok = rows_of(gather_dp(dispatch(tokens)))
    rows_grad = rows_of(gather_dp(dispatch(out_grad)))

    hidden_pre = jnp.einsum("erd,edf->erf", rows_tok, up_weight, preferred_element_type=jnp.float32)
    active = gelu_value(hidden_pre).astype(jnp.bfloat16)
    part = jnp.einsum("erf,efd->erd", active, down_weight, preferred_element_type=jnp.float32)
    part = jnp.split(part, rows * cols, axis=1)
    summed = scatter_dp([part[k * cols : (k + 1) * cols] for k in range(rows)]).astype(jnp.bfloat16)
    summed = summed.reshape(local_experts, owners, capacity, width).transpose(1, 0, 2, 3)
    returned = jnp.concatenate(exchange(summed), axis=0).reshape(slots, width)
    combined = jnp.einsum("rt,rd->td", place, returned, preferred_element_type=jnp.float32)
    combined = combined.astype(jnp.bfloat16)

    back_grad = jnp.einsum(
        "erd,efd->erf", rows_grad, down_weight, preferred_element_type=jnp.float32
    )
    pre_grad = (back_grad * gelu_slope(hidden_pre)).astype(jnp.bfloat16)
    down_part = jnp.einsum(
        "erf,erd->efd", active, rows_grad, preferred_element_type=jnp.float32
    ).astype(jnp.bfloat16)
    up_part = jnp.einsum(
        "erd,erf->edf", rows_tok, pre_grad, preferred_element_type=jnp.float32
    ).astype(jnp.bfloat16)
    return (combined, up_part, down_part)


def solution(mesh):
    in_specs = (
        P(("expert", "dp"), None),
        P(("expert", "dp")),
        P("expert", None, "dp"),
        P("expert", "dp", None),
        P(("expert", "dp"), None),
    )
    out_specs = (P(("expert", "dp"), None), P("expert", None, "dp"), P("expert", "dp", None))
    return jax.shard_map(
        on_device, mesh=mesh, in_specs=in_specs, out_specs=out_specs, check_vma=False
    )
```

```python
import math

import jax
import jax.numpy as jnp
from jax import lax
from jax.sharding import PartitionSpec as P

gelu_scale = math.sqrt(2.0 / math.pi)
cubic_term = 0.044715


def gelu_value(values):
    inner_arg = gelu_scale * (values + cubic_term * values * values * values)
    return 0.5 * values * (1.0 + jnp.tanh(inner_arg))


def gelu_slope(values):
    tangent = jnp.tanh(gelu_scale * (values + cubic_term * values * values * values))
    return 0.5 * (1.0 + tangent) + 0.5 * values * (1.0 - tangent * tangent) * gelu_scale * (
        1.0 + 3.0 * cubic_term * values * values
    )


def grid_of(n):
    cols = 1
    while cols * cols * 4 <= n and n % (cols * 2) == 0:
        cols *= 2
    return n // cols, cols


def ring_z(value, step):
    n = lax.axis_size("dp")
    rows, cols = grid_of(n)
    perm = [(i, ((i // cols + step) % rows) * cols + i % cols) for i in range(n)]
    return lax.ppermute(value, "dp", perm)


def ring_y(value, step):
    n = lax.axis_size("dp")
    cols = grid_of(n)[1]
    perm = [(i, i // cols * cols + (i % cols + step) % cols) for i in range(n)]
    return lax.ppermute(value, "dp", perm)


def swap_expert(value, mask):
    n = lax.axis_size("expert")
    return lax.ppermute(value, "expert", [(i, i ^ mask) for i in range(n)])


def exchange(packed):
    return [packed[0]] + [swap_expert(packed[m], m) for m in range(1, packed.shape[0])]


def after(value, *earlier):
    return lax.optimization_barrier((value, *earlier))[0]


def gather_dp(block):
    rows, cols = grid_of(lax.axis_size("dp"))
    half = block.shape[0] // 2
    blocks = []
    for k in range(rows):
        if k > 0:
            block = ring_z(block, 1)
        line = [block]
        if cols == 2 and k > 0 and k == rows - 1 and half > 0:
            low = ring_y(block[:half], 1)
            high = ring_z(blocks[k - 1][1][half:], 1)
            line.append(jnp.concatenate([low, high], axis=0))
        else:
            for _ in range(cols - 1):
                line.append(ring_y(line[-1], 1))
        blocks.append(line)
    return blocks


def scatter_dp(parts):
    rows, cols = grid_of(lax.axis_size("dp"))
    parts = [list(line) for line in parts]
    half = parts[0][0].shape[0] // 2

    def moved(ring, value):
        return ring(value.astype(jnp.bfloat16), -1).astype(jnp.float32)

    total = None
    for k in reversed(range(rows)):
        if cols == 2 and k > 0 and k == rows - 1 and half > 0:
            low = moved(ring_y, parts[k][1][:half]) + parts[k][0][:half]
            high = moved(ring_z, parts[k][1][half:]) + parts[k - 1][1][half:]
            line = jnp.concatenate([low, parts[k][0][half:]], axis=0)
            parts[k - 1][1] = jnp.concatenate([parts[k - 1][1][:half], high], axis=0)
        else:
            line = parts[k][cols - 1]
            for j in reversed(range(cols - 1)):
                line = moved(ring_y, line) + parts[k][j]
        total = line if total is None else moved(ring_z, total) + line
    return total


def on_device(tokens, expert_ids, up_weight, down_weight, out_grad):
    owners = lax.axis_size("expert")
    rows, cols = grid_of(lax.axis_size("dp"))
    local_experts = up_weight.shape[0]
    all_experts = owners * local_experts
    tok_rows, width = tokens.shape
    capacity = 5 * tok_rows // (4 * all_experts)
    slots = all_experts * capacity
    me = lax.axis_index("expert")
    index = jnp.arange(tok_rows, dtype=jnp.int32)
    earlier = (expert_ids[:, None] == expert_ids[None, :]) & (index[:, None] < index[None, :])
    slot_index = jnp.sum(earlier.astype(jnp.int32), axis=0)
    owner_id = expert_ids // local_experts
    local_id = expert_ids % local_experts
    target = ((owner_id ^ me) * local_experts + local_id) * capacity + slot_index
    place = (target[None, :] == jnp.arange(slots, dtype=jnp.int32)[:, None]).astype(jnp.bfloat16)

    def dispatch(values):
        packed = jnp.dot(place, values, preferred_element_type=jnp.float32).astype(values.dtype)
        got = exchange(packed.reshape(owners, local_experts, capacity, width))
        return jnp.stack(got, axis=1).reshape(local_experts, owners * capacity, width)

    def rows_of(blocks):
        return jnp.concatenate([b for line in blocks for b in line], axis=1)

    blocks_tok = gather_dp(dispatch(tokens))
    rows_tok = rows_of(blocks_tok)
    block_grad = after(dispatch(out_grad), blocks_tok[rows - 1][0])
    rows_grad = rows_of(gather_dp(block_grad))

    hidden_pre = jnp.einsum("erd,edf->erf", rows_tok, up_weight, preferred_element_type=jnp.float32)
    hidden_pre = lax.optimization_barrier(hidden_pre)
    active = gelu_value(hidden_pre).astype(jnp.bfloat16)
    active, slope = lax.optimization_barrier((active, gelu_slope(hidden_pre)))
    part = jnp.einsum("erf,efd->erd", active, down_weight, preferred_element_type=jnp.float32)
    part = jnp.split(part, rows * cols, axis=1)
    summed = scatter_dp([part[k * cols : (k + 1) * cols] for k in range(rows)]).astype(jnp.bfloat16)
    summed = summed.reshape(local_experts, owners, capacity, width).transpose(1, 0, 2, 3)
    returned = jnp.concatenate(exchange(summed), axis=0).reshape(slots, width)
    combined = jnp.einsum("rt,rd->td", place, returned, preferred_element_type=jnp.float32)
    combined = combined.astype(jnp.bfloat16)

    back_grad = jnp.einsum(
        "erd,efd->erf", rows_grad, down_weight, preferred_element_type=jnp.float32
    )
    pre_grad = lax.optimization_barrier((back_grad * slope).astype(jnp.bfloat16))
    down_part = jnp.einsum(
        "erf,erd->efd", active, rows_grad, preferred_element_type=jnp.float32
    ).astype(jnp.bfloat16)
    up_part = jnp.einsum(
        "erd,erf->edf", rows_tok, pre_grad, preferred_element_type=jnp.float32
    ).astype(jnp.bfloat16)
    return (combined, up_part, down_part)


def solution(mesh):
    in_specs = (
        P(("expert", "dp"), None),
        P(("expert", "dp")),
        P("expert", None, "dp"),
        P("expert", "dp", None),
        P(("expert", "dp"), None),
    )
    out_specs = (P(("expert", "dp"), None), P("expert", None, "dp"), P("expert", "dp", None))
    return jax.shard_map(
        on_device, mesh=mesh, in_specs=in_specs, out_specs=out_specs, check_vma=False
    )
```

```python
import math

import jax
import jax.numpy as jnp
from jax import lax
from jax.sharding import PartitionSpec as P

gelu_scale = math.sqrt(2.0 / math.pi)
cubic_term = 0.044715


def gelu_value(values):
    inner_arg = gelu_scale * (values + cubic_term * values * values * values)
    return 0.5 * values * (1.0 + jnp.tanh(inner_arg))


def gelu_slope(values):
    tangent = jnp.tanh(gelu_scale * (values + cubic_term * values * values * values))
    return 0.5 * (1.0 + tangent) + 0.5 * values * (1.0 - tangent * tangent) * gelu_scale * (
        1.0 + 3.0 * cubic_term * values * values
    )


def grid_of(n):
    cols = 1
    while cols * cols * 4 <= n and n % (cols * 2) == 0:
        cols *= 2
    return n // cols, cols


def ring_z(value, step):
    n = lax.axis_size("dp")
    rows, cols = grid_of(n)
    perm = [(i, ((i // cols + step) % rows) * cols + i % cols) for i in range(n)]
    return lax.ppermute(value, "dp", perm)


def ring_y(value, step):
    n = lax.axis_size("dp")
    cols = grid_of(n)[1]
    perm = [(i, i // cols * cols + (i % cols + step) % cols) for i in range(n)]
    return lax.ppermute(value, "dp", perm)


def swap_expert(value, mask):
    n = lax.axis_size("expert")
    return lax.ppermute(value, "expert", [(i, i ^ mask) for i in range(n)])


def exchange(packed):
    return [packed[0]] + [swap_expert(packed[m], m) for m in range(1, packed.shape[0])]


def gather_dp(block):
    rows, cols = grid_of(lax.axis_size("dp"))
    half = block.shape[0] // 2
    blocks = []
    for k in range(rows):
        if k > 0:
            block = ring_z(block, 1)
        line = [block]
        if cols == 2 and k > 0 and k == rows - 1 and half > 0:
            low = ring_y(block[:half], 1)
            high = ring_z(blocks[k - 1][1][half:], 1)
            line.append(jnp.concatenate([low, high], axis=0))
        else:
            for _ in range(cols - 1):
                line.append(ring_y(line[-1], 1))
        blocks.append(line)
    return blocks


def scatter_dp(parts):
    rows, cols = grid_of(lax.axis_size("dp"))
    parts = [list(line) for line in parts]
    half = parts[0][0].shape[0] // 2

    def moved(ring, value):
        return ring(value.astype(jnp.bfloat16), -1).astype(jnp.float32)

    total = None
    for k in reversed(range(rows)):
        if cols == 2 and k > 0 and k == rows - 1 and half > 0:
            low = moved(ring_y, parts[k][1][:half]) + parts[k][0][:half]
            high = moved(ring_z, parts[k][1][half:]) + parts[k - 1][1][half:]
            line = jnp.concatenate([low, parts[k][0][half:]], axis=0)
            parts[k - 1][1] = jnp.concatenate([parts[k - 1][1][:half], high], axis=0)
        else:
            line = parts[k][cols - 1]
            for j in reversed(range(cols - 1)):
                line = moved(ring_y, line) + parts[k][j]
        total = line if total is None else moved(ring_z, total) + line
    return total


def on_device(tokens, expert_ids, up_weight, down_weight, out_grad):
    owners = lax.axis_size("expert")
    rows, cols = grid_of(lax.axis_size("dp"))
    local_experts = up_weight.shape[0]
    all_experts = owners * local_experts
    tok_rows, width = tokens.shape
    capacity = 5 * tok_rows // (4 * all_experts)
    slots = all_experts * capacity
    me = lax.axis_index("expert")
    index = jnp.arange(tok_rows, dtype=jnp.int32)
    earlier = (expert_ids[:, None] == expert_ids[None, :]) & (index[:, None] < index[None, :])
    slot_index = jnp.sum(earlier.astype(jnp.int32), axis=0)
    owner_id = expert_ids // local_experts
    local_id = expert_ids % local_experts
    target = ((owner_id ^ me) * local_experts + local_id) * capacity + slot_index
    place = (target[None, :] == jnp.arange(slots, dtype=jnp.int32)[:, None]).astype(jnp.bfloat16)

    def dispatch(values):
        packed = jnp.dot(place, values, preferred_element_type=jnp.float32).astype(values.dtype)
        got = exchange(packed.reshape(owners, local_experts, capacity, width))
        return jnp.stack(got, axis=1).reshape(local_experts, owners * capacity, width)

    def rows_of(blocks):
        return jnp.concatenate([b for line in blocks for b in line], axis=1)

    blocks_tok = gather_dp(dispatch(tokens))
    rows_tok = rows_of(blocks_tok)
    rows_grad = rows_of(gather_dp(dispatch(out_grad)))

    hidden_pre = jnp.einsum("erd,edf->erf", rows_tok, up_weight, preferred_element_type=jnp.float32)
    hidden_pre = lax.optimization_barrier(hidden_pre)
    active = gelu_value(hidden_pre).astype(jnp.bfloat16)
    active, slope = lax.optimization_barrier((active, gelu_slope(hidden_pre)))
    part = jnp.einsum("erf,efd->erd", active, down_weight, preferred_element_type=jnp.float32)
    part = jnp.split(part, rows * cols, axis=1)
    halves = 2 if local_experts % 2 == 0 else 1
    count = local_experts // halves
    returned = []
    for first in range(0, local_experts, count):
        piece = [p[first : first + count] for p in part]
        summed = scatter_dp([piece[k * cols : (k + 1) * cols] for k in range(rows)])
        summed = summed.astype(jnp.bfloat16).reshape(count, owners, capacity, width)
        returned.append(jnp.stack(exchange(summed.transpose(1, 0, 2, 3))))
    returned = jnp.concatenate(returned, axis=1).reshape(slots, width)
    combined = jnp.einsum("rt,rd->td", place, returned, preferred_element_type=jnp.float32)
    combined = combined.astype(jnp.bfloat16)

    back_grad = jnp.einsum(
        "erd,efd->erf", rows_grad, down_weight, preferred_element_type=jnp.float32
    )
    pre_grad = lax.optimization_barrier((back_grad * slope).astype(jnp.bfloat16))
    down_part = jnp.einsum(
        "erf,erd->efd", active, rows_grad, preferred_element_type=jnp.float32
    ).astype(jnp.bfloat16)
    up_part = jnp.einsum(
        "erd,erf->edf", rows_tok, pre_grad, preferred_element_type=jnp.float32
    ).astype(jnp.bfloat16)
    return (combined, up_part, down_part)


def solution(mesh):
    in_specs = (
        P(("expert", "dp"), None),
        P(("expert", "dp")),
        P("expert", None, "dp"),
        P("expert", "dp", None),
        P(("expert", "dp"), None),
    )
    out_specs = (P(("expert", "dp"), None), P("expert", None, "dp"), P("expert", "dp", None))
    return jax.shard_map(
        on_device, mesh=mesh, in_specs=in_specs, out_specs=out_specs, check_vma=False
    )
```

```python
import math

import jax
import jax.numpy as jnp
from jax import lax
from jax.sharding import PartitionSpec as P

gelu_scale = math.sqrt(2.0 / math.pi)
cubic_term = 0.044715


def gelu_value(values):
    inner_arg = gelu_scale * (values + cubic_term * values * values * values)
    return 0.5 * values * (1.0 + jnp.tanh(inner_arg))


def gelu_slope(values):
    tangent = jnp.tanh(gelu_scale * (values + cubic_term * values * values * values))
    return 0.5 * (1.0 + tangent) + 0.5 * values * (1.0 - tangent * tangent) * gelu_scale * (
        1.0 + 3.0 * cubic_term * values * values
    )


def after(value, *earlier):
    return lax.optimization_barrier((value, *earlier))[0]


def grid_of(n):
    cols = 1
    while cols * cols * 4 <= n and n % (cols * 2) == 0:
        cols *= 2
    return n // cols, cols


def ring_z(value, step, name="z"):
    n = lax.axis_size("dp")
    rows, cols = grid_of(n)
    perm = [(i, ((i // cols + step) % rows) * cols + i % cols) for i in range(n)]
    with jax.named_scope(name):
        return lax.ppermute(value, "dp", perm)


def ring_y(value, step, name="y"):
    n = lax.axis_size("dp")
    cols = grid_of(n)[1]
    perm = [(i, i // cols * cols + (i % cols + step) % cols) for i in range(n)]
    with jax.named_scope(name):
        return lax.ppermute(value, "dp", perm)


def swap_expert(value, mask, name="swap"):
    n = lax.axis_size("expert")
    with jax.named_scope(f"{name}_x{mask}"):
        return lax.ppermute(value, "expert", [(i, i ^ mask) for i in range(n)])


def exchange(packed, name):
    return [packed[0]] + [swap_expert(packed[m], m, name) for m in range(1, packed.shape[0])]


def gather_step(blocks, k, name, hold=(), last_over_z=False):
    rows, cols = grid_of(lax.axis_size("dp"))
    size = blocks[0][0].shape[0]
    half = size // 32 * 16 if size % 8 == 0 and size >= 32 else size // 2
    here = blocks[k][0]
    beyond = blocks[max(k, 1) - 1][-1][half:]
    wait = (*hold, *([blocks[k - 1][-1]] if k > 0 else []))
    if wait:
        here, beyond, *_ = lax.optimization_barrier((here, beyond, *wait))
    if cols == 2 and k > 0 and k == rows - 1 and half > 0:
        if last_over_z:
            blocks[k].append(ring_z(after(blocks[k - 1][1], *hold), 1, f"{name}_z{k + 1}"))
            return blocks[k][1:]
        low = ring_y(here[:half], 1, f"{name}_y{k}")
        high = ring_z(beyond, 1, f"{name}_z{k + 1}")
        blocks[k].append(jnp.concatenate([low, high], axis=0))
        return [low, high]
    if k < rows - 1:
        blocks.append([ring_z(here, 1, f"{name}_z{k + 1}")])
    for j in range(cols - 1):
        blocks[k].append(ring_y(here if j == 0 else blocks[k][j], 1, f"{name}_y{k}"))
    return [blocks[k][-1], *(line[0] for line in blocks[k + 1 : k + 2])]


def cross(chunks, name, hold=()):
    if hold:
        chunks = after(chunks, *hold)
    pairs = chunks.shape[0] // 2
    return [chunks[:2]] + [
        swap_expert(chunks[2 * q : 2 * q + 2], 2 * q, name) for q in range(1, pairs)
    ]


def settle(got, name, hold=()):
    if hold:
        got = lax.optimization_barrier((*got, *hold))[: len(got)]
    back = swap_expert(jnp.stack([g[1] for g in got]), 1, name)
    return [c for q in range(len(got)) for c in (got[q][0], back[q])], back


def on_device(tokens, expert_ids, up_weight, down_weight, out_grad):
    owners = lax.axis_size("expert")
    rows, cols = grid_of(lax.axis_size("dp"))
    local_experts = up_weight.shape[0]
    all_experts = owners * local_experts
    tok_rows, width = tokens.shape
    capacity = 5 * tok_rows // (4 * all_experts)
    slots = all_experts * capacity
    me = lax.axis_index("expert")
    index = jnp.arange(tok_rows, dtype=jnp.int32)
    earlier = (expert_ids[:, None] == expert_ids[None, :]) & (index[:, None] < index[None, :])
    slot_index = jnp.sum(earlier.astype(jnp.int32), axis=0)
    owner_id = expert_ids // local_experts
    local_id = expert_ids % local_experts
    target = ((owner_id ^ me) * local_experts + local_id) * capacity + slot_index
    place = (target[None, :] == jnp.arange(slots, dtype=jnp.int32)[:, None]).astype(jnp.bfloat16)

    def pack(values):
        packed = jnp.dot(place, values, preferred_element_type=jnp.float32).astype(values.dtype)
        return packed.reshape(owners, local_experts, capacity, width)

    def block_of(got):
        return jnp.stack(got, axis=1).reshape(local_experts, owners * capacity, width)

    slot_iota = jnp.arange(slots, dtype=jnp.int32)
    row_of_slot = (
        (slot_iota // capacity % local_experts) * owners + slot_iota // (local_experts * capacity)
    ) * capacity + slot_iota % capacity
    reorder = (row_of_slot[:, None] == slot_iota[None, :]).astype(jnp.bfloat16)

    def pick(spec, onehot, values):
        found = jnp.einsum(spec, onehot, values, preferred_element_type=jnp.float32)
        return found.astype(jnp.bfloat16)

    def in_chunks(line):
        shape = (owners, local_experts * capacity, width)
        return jnp.stack([v.reshape(shape) for v in line], axis=1)

    def by_column(got):
        return [jnp.concatenate([g[j] for g in got], axis=0) for j in range(cols)]

    digits = jnp.stack([target // 256, target % 256]).astype(jnp.bfloat16)
    digits = jnp.pad(digits, ((0, 6), (0, width - tok_rows)))
    blocks_tok = [[jnp.concatenate([tokens, digits], axis=0)]]
    packed_grad = pack(out_grad)
    came, crossed_tok = [], []
    for k in range(rows):
        came.append(gather_step(blocks_tok, k, "tok", came[-1] if came else ()))
        if k == 0:
            got_grad = exchange(packed_grad, "grad")
            got_grad = lax.optimization_barrier((*got_grad, *came[k]))[: len(got_grad)]
            blocks_grad = [[block_of(got_grad)]]
        gather_step(blocks_grad, k, "grad", came[k], True)
    for k in range(rows):
        line = []
        for block in blocks_tok[k]:
            at = block[tok_rows : tok_rows + 2, :tok_rows].astype(jnp.int32)
            at = at[0] * 256 + at[1]
            at = (at[None, :] == slot_iota[:, None]).astype(jnp.bfloat16)
            line.append(pick("rt,td->rd", at, block[:tok_rows]))
        crossed_tok.append(cross(in_chunks(line), f"tok{k}"))

    rows_tok, active, slope, parts = [], [], [], []
    for k in range(rows):
        got, settled = settle(crossed_tok[k], f"tok{k}", came[k + 1] if k + 1 < rows else ())
        rows_k = [
            pick("cr,cd->rd", reorder, v).reshape(local_experts, owners * capacity, width)
            for v in by_column(got)
        ]
        rows_k = jnp.concatenate(rows_k, axis=1)
        hidden_k = jnp.einsum(
            "erd,edf->erf", rows_k, up_weight, preferred_element_type=jnp.float32
        )
        hidden_k = lax.optimization_barrier(hidden_k)
        active_k, slope_k = lax.optimization_barrier(
            (gelu_value(hidden_k).astype(jnp.bfloat16), gelu_slope(hidden_k))
        )
        part_k = jnp.einsum(
            "erf,efd->erd", active_k, down_weight, preferred_element_type=jnp.float32
        )
        parts.append(part_k.reshape(local_experts, cols, owners * capacity, width))
        rows_tok.append(rows_k)
        active.append(active_k)
        slope.append(slope_k)

    over_y = []

    def column_sum(k):
        total = parts[k][:, cols - 1].astype(jnp.bfloat16)
        if k == 0 and over_y:
            total = after(total, over_y[-1])
        for j in reversed(range(cols - 1)):
            over_y.append(ring_y(total, -1, f"out_y{k}"))
            total = over_y[-1].astype(jnp.float32) + parts[k][:, j]
            if j > 0:
                total = total.astype(jnp.bfloat16)
        return total.astype(jnp.float32)

    sums = [column_sum(k) for k in range(1, rows)]
    sums = [column_sum(0), *sums]
    summed, over_z = sums[0], []
    for ks, step in ((range(rows // 2, 0, -1), -1), (range(rows // 2 + 1, rows), 1)):
        total = None
        for k in ks:
            total = sums[k] if total is None else total + sums[k]
            over_z.append(ring_z(total.astype(jnp.bfloat16), step, f"out_z{k}"))
            total = over_z[-1].astype(jnp.float32)
        if total is not None:
            summed = summed + total
    summed = summed.astype(jnp.bfloat16)
    summed = pick("cr,rd->cd", reorder, summed.reshape(slots, width))
    returned = exchange(summed.reshape(owners, local_experts * capacity, width), "back")
    returned = jnp.concatenate(returned, axis=0)
    combined = pick("rt,rd->td", place, returned)

    rows_grad = jnp.concatenate([b for line in blocks_grad for b in line], axis=1)
    rows_tok = jnp.concatenate(rows_tok, axis=1)
    active = jnp.concatenate(active, axis=1)
    slope = jnp.concatenate(slope, axis=1)

    back_grad = jnp.einsum(
        "erd,efd->erf", rows_grad, down_weight, preferred_element_type=jnp.float32
    )
    pre_grad = lax.optimization_barrier((back_grad * slope).astype(jnp.bfloat16))
    down_part = jnp.einsum(
        "erf,erd->efd", active, rows_grad, preferred_element_type=jnp.float32
    ).astype(jnp.bfloat16)
    up_part = jnp.einsum(
        "erd,erf->edf", rows_tok, pre_grad, preferred_element_type=jnp.float32
    ).astype(jnp.bfloat16)
    return (combined, up_part, down_part)


def solution(mesh):
    in_specs = (
        P(("expert", "dp"), None),
        P(("expert", "dp")),
        P("expert", None, "dp"),
        P("expert", "dp", None),
        P(("expert", "dp"), None),
    )
    out_specs = (P(("expert", "dp"), None), P("expert", None, "dp"), P("expert", "dp", None))
    return jax.shard_map(
        on_device, mesh=mesh, in_specs=in_specs, out_specs=out_specs, check_vma=False
    )
```

```python
import math

import jax
import jax.numpy as jnp
from jax import lax
from jax.sharding import PartitionSpec as P

gelu_scale = math.sqrt(2.0 / math.pi)
cubic_term = 0.044715


def gelu_value(values):
    inner_arg = gelu_scale * (values + cubic_term * values * values * values)
    return 0.5 * values * (1.0 + jnp.tanh(inner_arg))


def gelu_slope(values):
    tangent = jnp.tanh(gelu_scale * (values + cubic_term * values * values * values))
    return 0.5 * (1.0 + tangent) + 0.5 * values * (1.0 - tangent * tangent) * gelu_scale * (
        1.0 + 3.0 * cubic_term * values * values
    )


def after(value, *earlier):
    return lax.optimization_barrier((value, *earlier))[0]


def grid_of(n):
    cols = 1
    while cols * cols * 4 <= n and n % (cols * 2) == 0:
        cols *= 2
    return n // cols, cols


def ring_z(value, step, name="z"):
    n = lax.axis_size("dp")
    rows, cols = grid_of(n)
    perm = [(i, ((i // cols + step) % rows) * cols + i % cols) for i in range(n)]
    with jax.named_scope(name):
        return lax.ppermute(value, "dp", perm)


def ring_y(value, step, name="y"):
    n = lax.axis_size("dp")
    cols = grid_of(n)[1]
    perm = [(i, i // cols * cols + (i % cols + step) % cols) for i in range(n)]
    with jax.named_scope(name):
        return lax.ppermute(value, "dp", perm)


def swap_expert(value, mask, name="swap"):
    n = lax.axis_size("expert")
    with jax.named_scope(f"{name}_x{mask}"):
        return lax.ppermute(value, "expert", [(i, i ^ mask) for i in range(n)])


def ring_z_to(value, step, mask, name):
    n, owners = lax.axis_size("dp"), lax.axis_size("expert")
    rows, cols = grid_of(n)
    perm = [
        (e * n + i, (e ^ mask) * n + ((i // cols + step) % rows) * cols + i % cols)
        for e in range(owners)
        for i in range(n)
    ]
    with jax.named_scope(f"{name}_x{mask}"):
        return lax.ppermute(value, ("expert", "dp"), perm)


def exchange(packed, name):
    return [packed[0]] + [swap_expert(packed[m], m, name) for m in range(1, packed.shape[0])]


def gather_step(blocks, k, name, hold=()):
    rows, cols = grid_of(lax.axis_size("dp"))
    size = blocks[0][0].shape[0]
    half = size // 32 * 16 if size % 8 == 0 and size >= 32 else size // 2
    here = blocks[k][0]
    beyond = blocks[max(k, 1) - 1][-1][half:]
    wait = (*hold, *([blocks[k - 1][-1]] if k > 0 else []))
    if wait:
        here, beyond, *_ = lax.optimization_barrier((here, beyond, *wait))
    if cols == 2 and k > 0 and k == rows - 1 and half > 0:
        high = ring_z(beyond, 1, f"{name}_z{k + 1}")
        low = ring_y(here[:half], 1, f"{name}_y{k}")
        blocks[k].append(jnp.concatenate([low, high], axis=0))
        return [low, high]
    if k < rows - 1:
        blocks.append([ring_z(here, 1, f"{name}_z{k + 1}")])
    for j in range(cols - 1):
        blocks[k].append(ring_y(here if j == 0 else blocks[k][j], 1, f"{name}_y{k}"))
    return [blocks[k][-1], *(line[0] for line in blocks[k + 1 : k + 2])]


def cross(chunks, name, hold=()):
    if hold:
        chunks = after(chunks, *hold)
    pairs = chunks.shape[0] // 2
    return [chunks[:2]] + [
        swap_expert(chunks[2 * q : 2 * q + 2], 2 * q, name) for q in range(1, pairs)
    ]


def settle(got, name, hold=()):
    if hold:
        got = lax.optimization_barrier((*got, *hold))[: len(got)]
    back = swap_expert(jnp.stack([g[1] for g in got]), 1, name)
    return [c for q in range(len(got)) for c in (got[q][0], back[q])]


def on_device(tokens, expert_ids, up_weight, down_weight, out_grad):
    owners = lax.axis_size("expert")
    rows, cols = grid_of(lax.axis_size("dp"))
    local_experts = up_weight.shape[0]
    all_experts = owners * local_experts
    tok_rows, width = tokens.shape
    capacity = 5 * tok_rows // (4 * all_experts)
    slots = all_experts * capacity
    me = lax.axis_index("expert")
    index = jnp.arange(tok_rows, dtype=jnp.int32)
    earlier = (expert_ids[:, None] == expert_ids[None, :]) & (index[:, None] < index[None, :])
    slot_index = jnp.sum(earlier.astype(jnp.int32), axis=0)
    owner_id = expert_ids // local_experts
    local_id = expert_ids % local_experts
    target = ((owner_id ^ me) * local_experts + local_id) * capacity + slot_index
    place = (target[None, :] == jnp.arange(slots, dtype=jnp.int32)[:, None]).astype(jnp.bfloat16)

    def pack(values):
        packed = jnp.dot(place, values, preferred_element_type=jnp.float32).astype(values.dtype)
        return packed.reshape(owners, local_experts, capacity, width)

    def block_of(got):
        return jnp.stack(got, axis=1).reshape(local_experts, owners * capacity, width)

    slot_iota = jnp.arange(slots, dtype=jnp.int32)
    row_of_slot = (
        (slot_iota // capacity % local_experts) * owners + slot_iota // (local_experts * capacity)
    ) * capacity + slot_iota % capacity
    reorder = (row_of_slot[:, None] == slot_iota[None, :]).astype(jnp.bfloat16)

    def pick(spec, onehot, values):
        found = jnp.einsum(spec, onehot, values, preferred_element_type=jnp.float32)
        return found.astype(jnp.bfloat16)

    def in_chunks(line):
        shape = (owners, local_experts * capacity, width)
        return jnp.stack([v.reshape(shape) for v in line], axis=1)

    def by_column(got):
        return [jnp.concatenate([g[j] for g in got], axis=0) for j in range(cols)]

    digits = jnp.stack([target // 256, target % 256]).astype(jnp.bfloat16)
    digits = jnp.pad(digits, ((0, 6), (0, width - tok_rows)))
    blocks_tok = [[jnp.concatenate([tokens, digits], axis=0)]]
    packed_grad = pack(out_grad)
    came, crossed_tok, blocks_grad = [], [], []
    for k in range(rows):
        came.append(gather_step(blocks_tok, k, "tok", came[-1] if came else ()))
        if k == 0:
            got_grad = exchange(packed_grad, "grad")
            got_grad = lax.optimization_barrier((*got_grad, *came[k]))[: len(got_grad)]
            blocks_grad.append([block_of(got_grad)])
        line = []
        for block in blocks_tok[k]:
            at = block[tok_rows : tok_rows + 2, :tok_rows].astype(jnp.int32)
            at = at[0] * 256 + at[1]
            at = (at[None, :] == slot_iota[:, None]).astype(jnp.bfloat16)
            line.append(pick("rt,td->rd", at, block[:tok_rows]))
        crossed_tok.append(cross(in_chunks(line), f"tok{k}"))
        if 0 < k:
            gather_step(blocks_grad, k - 1, "grad", came[k])

    rows_tok, active, slope, parts = [], [], [], []
    for k in range(rows):
        got = settle(crossed_tok[k], f"tok{k}", came[k + 1] if k + 1 < rows else ())
        rows_k = [
            pick("cr,cd->rd", reorder, v).reshape(local_experts, owners * capacity, width)
            for v in by_column(got)
        ]
        rows_k = jnp.concatenate(rows_k, axis=1)
        hidden_k = jnp.einsum(
            "erd,edf->erf", rows_k, up_weight, preferred_element_type=jnp.float32
        )
        hidden_k = lax.optimization_barrier(hidden_k)
        active_k, slope_k = lax.optimization_barrier(
            (gelu_value(hidden_k).astype(jnp.bfloat16), gelu_slope(hidden_k))
        )
        part_k = jnp.einsum(
            "erf,efd->erd", active_k, down_weight, preferred_element_type=jnp.float32
        )
        parts.append(part_k.reshape(local_experts, cols, owners * capacity, width))
        rows_tok.append(rows_k)
        active.append(active_k)
        slope.append(slope_k)
    over_y, sums = {}, {}
    for k in [*range(1, rows), 0]:
        total = parts[k][:, cols - 1].astype(jnp.bfloat16)
        hold = over_y.get(1) if 1 < k == rows - 1 else over_y.get(rows // 2) if k == 0 else None
        if hold is not None:
            total = after(total, hold)
        for j in reversed(range(cols - 1)):
            over_y[k] = ring_y(total, -1, f"out_y{k}")
            total = over_y[k].astype(jnp.float32) + parts[k][:, j]
            if j > 0:
                total = total.astype(jnp.bfloat16)
        sums[k] = total.astype(jnp.float32)

    if cols == 2 and rows > 1:
        blocks_grad[-1].append(ring_z(blocks_grad[-2][1], 1, f"grad_z{rows}"))
    else:
        gather_step(blocks_grad, rows - 1, "grad")
    if rows - 1 in over_y:
        blocks_grad[-1][-1] = after(blocks_grad[-1][-1], over_y[rows - 1])
    rows_grad = jnp.concatenate([b for line in blocks_grad for b in line], axis=1)

    rows_tok = jnp.concatenate(rows_tok, axis=1)
    active = jnp.concatenate(active, axis=1)
    slope = jnp.concatenate(slope, axis=1)
    back_grad = jnp.einsum(
        "erd,efd->erf", rows_grad, down_weight, preferred_element_type=jnp.float32
    )
    pre_grad = lax.optimization_barrier((back_grad * slope).astype(jnp.bfloat16))
    down_part = jnp.einsum(
        "erf,erd->efd", active, rows_grad, preferred_element_type=jnp.float32
    ).astype(jnp.bfloat16)
    up_part = jnp.einsum(
        "erd,erf->edf", rows_tok, pre_grad, preferred_element_type=jnp.float32
    ).astype(jnp.bfloat16)

    def by_owner(total):
        total = pick("cr,rd->cd", reorder, total.astype(jnp.bfloat16).reshape(slots, width))
        return list(total.reshape(owners // 2, 2, local_experts * capacity, width))

    total = by_owner(sums[0])
    arrived = [
        [total[0]] + [swap_expert(total[q], 2 * q, "own") for q in range(1, owners // 2)]
    ]
    for ks, step in ((range(rows // 2, 0, -1), -1), (range(rows // 2 + 1, rows), 1)):
        total = None
        for k in ks:
            total = sums[k] if total is None else total + sums[k]
            if k == ks[-1]:
                total = by_owner(total)
                arrived.append(
                    [ring_z_to(t, step, 2 * q, f"out_z{k}") for q, t in enumerate(total)]
                )
            else:
                total = ring_z(total.astype(jnp.bfloat16), step, f"out_z{k}").astype(jnp.float32)
    total = [sum(t.astype(jnp.float32) for t in ts).astype(jnp.bfloat16) for ts in zip(*arrived)]
    back = swap_expert(jnp.stack([t[1] for t in total]), 1, "back")
    returned = jnp.concatenate([v for t, other in zip(total, back) for v in (t[0], other)], axis=0)
    combined = pick("rt,rd->td", place, returned)
    return (combined, up_part, down_part)


def solution(mesh):
    in_specs = (
        P(("expert", "dp"), None),
        P(("expert", "dp")),
        P("expert", None, "dp"),
        P("expert", "dp", None),
        P(("expert", "dp"), None),
    )
    out_specs = (P(("expert", "dp"), None), P("expert", None, "dp"), P("expert", "dp", None))
    return jax.shard_map(
        on_device, mesh=mesh, in_specs=in_specs, out_specs=out_specs, check_vma=False
    )
```

```python
import math

import jax
import jax.numpy as jnp
from jax import lax
from jax.sharding import PartitionSpec as P

gelu_scale = math.sqrt(2.0 / math.pi)
cubic_term = 0.044715


def gelu_value(values):
    inner_arg = gelu_scale * (values + cubic_term * values * values * values)
    return 0.5 * values * (1.0 + jnp.tanh(inner_arg))


def gelu_slope(values):
    tangent = jnp.tanh(gelu_scale * (values + cubic_term * values * values * values))
    return 0.5 * (1.0 + tangent) + 0.5 * values * (1.0 - tangent * tangent) * gelu_scale * (
        1.0 + 3.0 * cubic_term * values * values
    )


def after(value, *earlier):
    return lax.optimization_barrier((value, *earlier))[0]


def grid_of(n):
    cols = 1
    while cols * cols * 4 <= n and n % (cols * 2) == 0:
        cols *= 2
    return n // cols, cols


def ring_z(value, step, name="z"):
    n = lax.axis_size("dp")
    rows, cols = grid_of(n)
    perm = [(i, ((i // cols + step) % rows) * cols + i % cols) for i in range(n)]
    with jax.named_scope(name):
        return lax.ppermute(value, "dp", perm)


def ring_y(value, step, name="y"):
    n = lax.axis_size("dp")
    cols = grid_of(n)[1]
    perm = [(i, i // cols * cols + (i % cols + step) % cols) for i in range(n)]
    with jax.named_scope(name):
        return lax.ppermute(value, "dp", perm)


def swap_expert(value, mask, name="swap"):
    n = lax.axis_size("expert")
    with jax.named_scope(f"{name}_x{mask}"):
        return lax.ppermute(value, "expert", [(i, i ^ mask) for i in range(n)])


def ring_z_to(value, step, mask, name):
    n, owners = lax.axis_size("dp"), lax.axis_size("expert")
    rows, cols = grid_of(n)
    perm = [
        (e * n + i, (e ^ mask) * n + ((i // cols + step) % rows) * cols + i % cols)
        for e in range(owners)
        for i in range(n)
    ]
    with jax.named_scope(f"{name}_x{mask}"):
        return lax.ppermute(value, ("expert", "dp"), perm)


def exchange(packed, name):
    return [packed[0]] + [swap_expert(packed[m], m, name) for m in range(1, packed.shape[0])]


def gather_step(blocks, k, name, hold=()):
    rows, cols = grid_of(lax.axis_size("dp"))
    size = blocks[0][0].shape[0]
    half = size // 32 * 16 if size % 8 == 0 and size >= 32 else size // 2
    here = blocks[k][0]
    beyond = blocks[max(k, 1) - 1][-1][half:]
    wait = (*hold, *([blocks[k - 1][-1]] if k > 0 else []))
    if wait:
        here, beyond, *_ = lax.optimization_barrier((here, beyond, *wait))
    if cols == 2 and k > 0 and k == rows - 1 and half > 0:
        high = ring_z(beyond, 1, f"{name}_z{k + 1}")
        low = ring_y(here[:half], 1, f"{name}_y{k}")
        blocks[k].append(jnp.concatenate([low, high], axis=0))
        return [low, high]
    if k < rows - 1:
        blocks.append([ring_z(here, 1, f"{name}_z{k + 1}")])
    for j in range(cols - 1):
        blocks[k].append(ring_y(here if j == 0 else blocks[k][j], 1, f"{name}_y{k}"))
    return [blocks[k][-1], *(line[0] for line in blocks[k + 1 : k + 2])]


def cross(chunks, name, hold=()):
    if hold:
        chunks = after(chunks, *hold)
    pairs = chunks.shape[0] // 2
    return [chunks[:2]] + [
        swap_expert(chunks[2 * q : 2 * q + 2], 2 * q, name) for q in range(1, pairs)
    ]


def settle(got, name, hold=()):
    if hold:
        got = lax.optimization_barrier((*got, *hold))[: len(got)]
    back = swap_expert(jnp.stack([g[1] for g in got]), 1, name)
    return [c for q in range(len(got)) for c in (got[q][0], back[q])]


def on_device(tokens, expert_ids, up_weight, down_weight, out_grad):
    owners = lax.axis_size("expert")
    rows, cols = grid_of(lax.axis_size("dp"))
    local_experts = up_weight.shape[0]
    all_experts = owners * local_experts
    tok_rows, width = tokens.shape
    capacity = 5 * tok_rows // (4 * all_experts)
    slots = all_experts * capacity
    me = lax.axis_index("expert")
    index = jnp.arange(tok_rows, dtype=jnp.int32)
    earlier = (expert_ids[:, None] == expert_ids[None, :]) & (index[:, None] < index[None, :])
    slot_index = jnp.sum(earlier.astype(jnp.int32), axis=0)
    owner_id = expert_ids // local_experts
    local_id = expert_ids % local_experts
    target = ((owner_id ^ me) * local_experts + local_id) * capacity + slot_index
    place = (target[None, :] == jnp.arange(slots, dtype=jnp.int32)[:, None]).astype(jnp.bfloat16)

    def pack(values):
        packed = jnp.dot(place, values, preferred_element_type=jnp.float32).astype(values.dtype)
        return packed.reshape(owners, local_experts, capacity, width)

    def block_of(got):
        return jnp.stack(got, axis=1).reshape(local_experts, owners * capacity, width)

    slot_iota = jnp.arange(slots, dtype=jnp.int32)
    row_of_slot = (
        (slot_iota // capacity % local_experts) * owners + slot_iota // (local_experts * capacity)
    ) * capacity + slot_iota % capacity
    reorder = (row_of_slot[:, None] == slot_iota[None, :]).astype(jnp.bfloat16)

    def pick(spec, onehot, values):
        found = jnp.einsum(spec, onehot, values, preferred_element_type=jnp.float32)
        return found.astype(jnp.bfloat16)

    def in_chunks(line):
        shape = (owners, local_experts * capacity, width)
        return jnp.stack([v.reshape(shape) for v in line], axis=1)

    def by_column(got):
        return [jnp.concatenate([g[j] for g in got], axis=0) for j in range(cols)]

    digits = jnp.stack([target // 256, target % 256]).astype(jnp.bfloat16)
    digits = jnp.pad(digits, ((0, 6), (0, width - tok_rows)))
    blocks_tok = [[jnp.concatenate([tokens, digits], axis=0)]]
    packed_grad = pack(out_grad)
    came, crossed_tok, blocks_grad = [], [], []
    for k in range(rows):
        came.append(gather_step(blocks_tok, k, "tok", came[-1] if came else ()))
        if k == 0:
            got_grad = exchange(packed_grad, "grad")
            got_grad = lax.optimization_barrier((*got_grad, *came[k]))[: len(got_grad)]
            blocks_grad.append([block_of(got_grad)])
        line = []
        for block in blocks_tok[k]:
            at = block[tok_rows : tok_rows + 2, :tok_rows].astype(jnp.int32)
            at = at[0] * 256 + at[1]
            at = (at[None, :] == slot_iota[:, None]).astype(jnp.bfloat16)
            line.append(pick("rt,td->rd", at, block[:tok_rows]))
        crossed_tok.append(cross(in_chunks(line), f"tok{k}"))
        if 0 < k:
            gather_step(blocks_grad, k - 1, "grad", came[k])

    rows_tok, active, slope, parts = [], [], [], []
    for k in range(rows):
        got = settle(crossed_tok[k], f"tok{k}", came[k + 1] if k + 1 < rows else ())
        rows_k = [
            pick("cr,cd->rd", reorder, v).reshape(local_experts, owners * capacity, width)
            for v in by_column(got)
        ]
        rows_k = jnp.concatenate(rows_k, axis=1)
        hidden_k = jnp.einsum(
            "erd,edf->erf", rows_k, up_weight, preferred_element_type=jnp.float32
        )
        hidden_k = lax.optimization_barrier(hidden_k)
        active_k, slope_k = lax.optimization_barrier(
            (gelu_value(hidden_k).astype(jnp.bfloat16), gelu_slope(hidden_k))
        )
        part_k = jnp.einsum(
            "erf,efd->erd", active_k, down_weight, preferred_element_type=jnp.float32
        )
        parts.append(part_k.reshape(local_experts, cols, owners * capacity, width))
        rows_tok.append(rows_k)
        active.append(active_k)
        slope.append(slope_k)
    over_y, sums = {}, {}
    for k in [*range(1, rows), 0]:
        total = parts[k][:, cols - 1].astype(jnp.bfloat16)
        hold = over_y.get(1) if 1 < k == rows - 1 else over_y.get(rows // 2) if k == 0 else None
        if hold is not None:
            total = after(total, hold)
        for j in reversed(range(cols - 1)):
            over_y[k] = ring_y(total, -1, f"out_y{k}")
            total = over_y[k].astype(jnp.float32) + parts[k][:, j]
            if j > 0:
                total = total.astype(jnp.bfloat16)
        sums[k] = total.astype(jnp.float32)

    if cols == 2 and rows > 1:
        blocks_grad[-1].append(ring_z(blocks_grad[-2][1], 1, f"grad_z{rows}"))
    else:
        gather_step(blocks_grad, rows - 1, "grad")
    def by_owner(total):
        total = pick("cr,rd->cd", reorder, total.astype(jnp.bfloat16).reshape(slots, width))
        return list(total.reshape(owners // 2, 2, local_experts * capacity, width))

    total = by_owner(sums[0])
    arrived = [
        [total[0]] + [swap_expert(total[q], 2 * q, "own") for q in range(1, owners // 2)]
    ]
    over_z = None
    for ks, step in ((range(rows // 2, 0, -1), -1), (range(rows // 2 + 1, rows), 1)):
        total = None
        for k in ks:
            total = sums[k] if total is None else total + sums[k]
            if k == ks[-1]:
                total = by_owner(total)
                arrived.append(
                    [ring_z_to(t, step, 2 * q, f"out_z{k}") for q, t in enumerate(total)]
                )
            else:
                over_z = ring_z(total.astype(jnp.bfloat16), step, f"out_z{k}")
                total = over_z.astype(jnp.float32)
    if over_z is not None:
        blocks_grad[-1][-1] = after(blocks_grad[-1][-1], over_z)
    rows_grad = jnp.concatenate([b for line in blocks_grad for b in line], axis=1)

    rows_tok = jnp.concatenate(rows_tok, axis=1)
    active = jnp.concatenate(active, axis=1)
    slope = jnp.concatenate(slope, axis=1)
    back_grad = jnp.einsum(
        "erd,efd->erf", rows_grad, down_weight, preferred_element_type=jnp.float32
    )
    pre_grad = lax.optimization_barrier((back_grad * slope).astype(jnp.bfloat16))
    down_part = jnp.einsum(
        "erf,erd->efd", active, rows_grad, preferred_element_type=jnp.float32
    ).astype(jnp.bfloat16)
    up_part = jnp.einsum(
        "erd,erf->edf", rows_tok, pre_grad, preferred_element_type=jnp.float32
    ).astype(jnp.bfloat16)

    total = [sum(t.astype(jnp.float32) for t in ts).astype(jnp.bfloat16) for ts in zip(*arrived)]
    back = swap_expert(after(jnp.stack([t[1] for t in total]), up_part, down_part), 1, "back")
    returned = jnp.concatenate([v for t, other in zip(total, back) for v in (t[0], other)], axis=0)
    combined = pick("rt,rd->td", place, returned)
    return (combined, up_part, down_part)


def solution(mesh):
    in_specs = (
        P(("expert", "dp"), None),
        P(("expert", "dp")),
        P("expert", None, "dp"),
        P("expert", "dp", None),
        P(("expert", "dp"), None),
    )
    out_specs = (P(("expert", "dp"), None), P("expert", None, "dp"), P("expert", "dp", None))
    return jax.shard_map(
        on_device, mesh=mesh, in_specs=in_specs, out_specs=out_specs, check_vma=False
    )
```

```python
import math

import jax
import jax.numpy as jnp
from jax import lax
from jax.sharding import PartitionSpec as P

gelu_scale = math.sqrt(2.0 / math.pi)
cubic_term = 0.044715


def gelu_value(values):
    inner_arg = gelu_scale * (values + cubic_term * values * values * values)
    return 0.5 * values * (1.0 + jnp.tanh(inner_arg))


def gelu_slope(values):
    tangent = jnp.tanh(gelu_scale * (values + cubic_term * values * values * values))
    return 0.5 * (1.0 + tangent) + 0.5 * values * (1.0 - tangent * tangent) * gelu_scale * (
        1.0 + 3.0 * cubic_term * values * values
    )


def after(value, *earlier):
    return lax.optimization_barrier((value, *earlier))[0]


def grid_of(n):
    cols = 1
    while cols * cols * 4 <= n and n % (cols * 2) == 0:
        cols *= 2
    return n // cols, cols


def ring_z(value, step, name="z"):
    n = lax.axis_size("dp")
    rows, cols = grid_of(n)
    perm = [(i, ((i // cols + step) % rows) * cols + i % cols) for i in range(n)]
    with jax.named_scope(name):
        return lax.ppermute(value, "dp", perm)


def ring_y(value, step, name="y"):
    n = lax.axis_size("dp")
    cols = grid_of(n)[1]
    perm = [(i, i // cols * cols + (i % cols + step) % cols) for i in range(n)]
    with jax.named_scope(name):
        return lax.ppermute(value, "dp", perm)


def swap_expert(value, mask, name="swap"):
    n = lax.axis_size("expert")
    with jax.named_scope(f"{name}_x{mask}"):
        return lax.ppermute(value, "expert", [(i, i ^ mask) for i in range(n)])


def ring_z_to(value, step, mask, name):
    n, owners = lax.axis_size("dp"), lax.axis_size("expert")
    rows, cols = grid_of(n)
    perm = [
        (e * n + i, (e ^ mask) * n + ((i // cols + step) % rows) * cols + i % cols)
        for e in range(owners)
        for i in range(n)
    ]
    with jax.named_scope(f"{name}_x{mask}"):
        return lax.ppermute(value, ("expert", "dp"), perm)


def exchange(packed, name):
    return [packed[0]] + [swap_expert(packed[m], m, name) for m in range(1, packed.shape[0])]


def gather_step(blocks, k, name, hold=()):
    rows, cols = grid_of(lax.axis_size("dp"))
    size = blocks[0][0].shape[0]
    half = size // 32 * 16 if size % 8 == 0 and size >= 32 else size // 2
    here = blocks[k][0]
    beyond = blocks[max(k, 1) - 1][-1][half:]
    wait = (*hold, *([blocks[k - 1][-1]] if k > 0 else []))
    if wait:
        here, beyond, *_ = lax.optimization_barrier((here, beyond, *wait))
    if cols == 2 and k > 0 and k == rows - 1 and half > 0:
        high = ring_z(beyond, 1, f"{name}_z{k + 1}")
        low = ring_y(here[:half], 1, f"{name}_y{k}")
        blocks[k].append(jnp.concatenate([low, high], axis=0))
        return [low, high]
    if k < rows - 1:
        blocks.append([ring_z(here, 1, f"{name}_z{k + 1}")])
    for j in range(cols - 1):
        blocks[k].append(ring_y(here if j == 0 else blocks[k][j], 1, f"{name}_y{k}"))
    return [blocks[k][-1], *(line[0] for line in blocks[k + 1 : k + 2])]


def cross(chunks, name, hold=()):
    if hold:
        chunks = after(chunks, *hold)
    pairs = chunks.shape[0] // 2
    return [chunks[:2]] + [
        swap_expert(chunks[2 * q : 2 * q + 2], 2 * q, name) for q in range(1, pairs)
    ]


def settle(got, name, hold=()):
    if hold:
        got = lax.optimization_barrier((*got, *hold))[: len(got)]
    back = swap_expert(jnp.stack([g[1] for g in got]), 1, name)
    return [c for q in range(len(got)) for c in (got[q][0], back[q])]


def on_device(tokens, expert_ids, up_weight, down_weight, out_grad):
    owners = lax.axis_size("expert")
    rows, cols = grid_of(lax.axis_size("dp"))
    local_experts = up_weight.shape[0]
    all_experts = owners * local_experts
    tok_rows, width = tokens.shape
    capacity = 5 * tok_rows // (4 * all_experts)
    slots = all_experts * capacity
    me = lax.axis_index("expert")
    index = jnp.arange(tok_rows, dtype=jnp.int32)
    earlier = (expert_ids[:, None] == expert_ids[None, :]) & (index[:, None] < index[None, :])
    slot_index = jnp.sum(earlier.astype(jnp.int32), axis=0)
    owner_id = expert_ids // local_experts
    local_id = expert_ids % local_experts
    target = ((owner_id ^ me) * local_experts + local_id) * capacity + slot_index
    place = (target[None, :] == jnp.arange(slots, dtype=jnp.int32)[:, None]).astype(jnp.bfloat16)

    def pack(values):
        packed = jnp.dot(place, values, preferred_element_type=jnp.float32).astype(values.dtype)
        return packed.reshape(owners, local_experts, capacity, width)

    def block_of(got):
        return jnp.stack(got, axis=1).reshape(local_experts, owners * capacity, width)

    slot_iota = jnp.arange(slots, dtype=jnp.int32)
    row_of_slot = (
        (slot_iota // capacity % local_experts) * owners + slot_iota // (local_experts * capacity)
    ) * capacity + slot_iota % capacity
    reorder = (row_of_slot[:, None] == slot_iota[None, :]).astype(jnp.bfloat16)

    def pick(spec, onehot, values):
        found = jnp.einsum(spec, onehot, values, preferred_element_type=jnp.float32)
        return found.astype(jnp.bfloat16)

    def in_chunks(line):
        shape = (owners, local_experts * capacity, width)
        return jnp.stack([v.reshape(shape) for v in line], axis=1)

    def by_column(got):
        return [jnp.concatenate([g[j] for g in got], axis=0) for j in range(cols)]

    digits = jnp.stack([target // 256, target % 256]).astype(jnp.bfloat16)
    digits = jnp.pad(digits, ((0, 6), (0, width - tok_rows)))
    blocks_tok = [[jnp.concatenate([tokens, digits], axis=0)]]
    packed_grad = pack(out_grad)
    came, crossed_tok, blocks_grad = [], [], []
    for k in range(rows):
        came.append(gather_step(blocks_tok, k, "tok", came[-1] if came else ()))
        if k == 0:
            got_grad = exchange(packed_grad, "grad")
            got_grad = lax.optimization_barrier((*got_grad, *came[k]))[: len(got_grad)]
            blocks_grad.append([block_of(got_grad)])
        line = []
        for block in blocks_tok[k]:
            at = block[tok_rows : tok_rows + 2, :tok_rows].astype(jnp.int32)
            at = at[0] * 256 + at[1]
            at = (at[None, :] == slot_iota[:, None]).astype(jnp.bfloat16)
            line.append(pick("rt,td->rd", at, block[:tok_rows]))
        crossed_tok.append(cross(in_chunks(line), f"tok{k}"))
        if k < rows - 1:
            gather_step(blocks_grad, k, "grad", came[k])

    rows_tok, active, slope, parts = [], [], [], []
    for k in range(rows):
        got = settle(crossed_tok[k], f"tok{k}", came[k + 1] if k + 1 < rows else ())
        rows_k = [
            pick("cr,cd->rd", reorder, v).reshape(local_experts, owners * capacity, width)
            for v in by_column(got)
        ]
        rows_k = jnp.concatenate(rows_k, axis=1)
        hidden_k = jnp.einsum(
            "erd,edf->erf", rows_k, up_weight, preferred_element_type=jnp.float32
        )
        hidden_k = lax.optimization_barrier(hidden_k)
        active_k, slope_k = lax.optimization_barrier(
            (gelu_value(hidden_k).astype(jnp.bfloat16), gelu_slope(hidden_k))
        )
        part_k = jnp.einsum(
            "erf,efd->erd", active_k, down_weight, preferred_element_type=jnp.float32
        )
        parts.append(part_k.reshape(local_experts, cols, owners * capacity, width))
        rows_tok.append(rows_k)
        active.append(active_k)
        slope.append(slope_k)
    over_y, sums = {}, {}
    for k in [*range(1, rows), 0]:
        total = parts[k][:, cols - 1].astype(jnp.bfloat16)
        hold = over_y.get(1) if 1 < k == rows - 1 else over_y.get(rows // 2) if k == 0 else None
        if hold is not None:
            total = after(total, hold)
        for j in reversed(range(cols - 1)):
            over_y[k] = ring_y(total, -1, f"out_y{k}")
            total = over_y[k].astype(jnp.float32) + parts[k][:, j]
            if j > 0:
                total = total.astype(jnp.bfloat16)
        sums[k] = total.astype(jnp.float32)

    if cols == 2 and rows > 1:
        blocks_grad[-1].append(ring_z(blocks_grad[-2][1], 1, f"grad_z{rows}"))
    else:
        gather_step(blocks_grad, rows - 1, "grad")
    def by_owner(total):
        total = pick("cr,rd->cd", reorder, total.astype(jnp.bfloat16).reshape(slots, width))
        return list(total.reshape(owners // 2, 2, local_experts * capacity, width))

    total = by_owner(sums[0])
    arrived = [
        [total[0]] + [swap_expert(total[q], 2 * q, "own") for q in range(1, owners // 2)]
    ]
    over_z = None
    for ks, step in ((range(rows // 2, 0, -1), -1), (range(rows // 2 + 1, rows), 1)):
        total = None
        for k in ks:
            total = sums[k] if total is None else total + sums[k]
            if k == ks[-1]:
                total = by_owner(total)
                arrived.append(
                    [ring_z_to(t, step, 2 * q, f"out_z{k}") for q, t in enumerate(total)]
                )
            else:
                over_z = ring_z(total.astype(jnp.bfloat16), step, f"out_z{k}")
                total = over_z.astype(jnp.float32)
    if over_z is not None:
        blocks_grad[-1][-1] = after(blocks_grad[-1][-1], over_z)
    rows_grad = jnp.concatenate([b for line in blocks_grad for b in line], axis=1)

    rows_tok = jnp.concatenate(rows_tok, axis=1)
    active = jnp.concatenate(active, axis=1)
    slope = jnp.concatenate(slope, axis=1)
    back_grad = jnp.einsum(
        "erd,efd->erf", rows_grad, down_weight, preferred_element_type=jnp.float32
    )
    pre_grad = lax.optimization_barrier((back_grad * slope).astype(jnp.bfloat16))
    down_part = jnp.einsum(
        "erf,erd->efd", active, rows_grad, preferred_element_type=jnp.float32
    ).astype(jnp.bfloat16)
    up_part = jnp.einsum(
        "erd,erf->edf", rows_tok, pre_grad, preferred_element_type=jnp.float32
    ).astype(jnp.bfloat16)

    total = [sum(t.astype(jnp.float32) for t in ts).astype(jnp.bfloat16) for ts in zip(*arrived)]
    back = swap_expert(after(jnp.stack([t[1] for t in total]), up_part, down_part), 1, "back")
    returned = jnp.concatenate([v for t, other in zip(total, back) for v in (t[0], other)], axis=0)
    combined = pick("rt,rd->td", place, returned)
    return (combined, up_part, down_part)


def solution(mesh):
    in_specs = (
        P(("expert", "dp"), None),
        P(("expert", "dp")),
        P("expert", None, "dp"),
        P("expert", "dp", None),
        P(("expert", "dp"), None),
    )
    out_specs = (P(("expert", "dp"), None), P("expert", None, "dp"), P("expert", "dp", None))
    return jax.shard_map(
        on_device, mesh=mesh, in_specs=in_specs, out_specs=out_specs, check_vma=False
    )
```
